32 devices in a mesh: frames: 4 (over x, core), rows: 8 (over z, y).
Axes of the slice: x: 2, y: 2, z: 4, core: 2. Of those that a mesh axis runs over, the one named last changes fastest.
Arguments:
- clip_in: bfloat16 [16, 32, 64, 256], P('frames', 'rows'), may hold values from -6 to 6
- kernel_one: bfloat16 [3, 3, 3, 64, 64], replicated, may hold values from -0.15625 to 0.15625
- bias_one: float32 [64], replicated, may hold values from -3 to 3
- kernel_two: bfloat16 [3, 3, 3, 64, 64], replicated, may hold values from -0.3125 to 0.3125
- cotangent: bfloat16 [16, 32, 64, 256], P('frames', 'rows'), may hold values from -6 to 6
Outputs:
- block_out: bfloat16 [16, 32, 64, 256], P('frames', 'rows')
- grad_input: bfloat16 [16, 32, 64, 256], P('frames', 'rows')
- grad_first: float32 [3, 3, 3, 64, 64], replicated
- grad_second: float32 [3, 3, 3, 64, 64], replicated
- grad_bias: float32 [64], replicated
The draws below stay inside these ranges and needn't reach their ends.
All inputs are finite; a program needn't handle non-finite values.
Results may differ from the reference program's by a relative error of at most 0.0065.
Values may be sent and summed in bfloat16 or wider, within the bound.
A program may use at most 64 MiB of HBM per device.

```python
import math
import jax
import jax.numpy as jnp
from jax import lax

C = 64
COLS = 256
FRAMES = 16
ROWS = 32


def shard_levels(key, shape, cuts, low, largest):
    gain = 1.0
    for dim, blocks in cuts:
        heights = jax.random.uniform(jax.random.fold_in(jax.random.fold_in(key, 6), dim), (blocks,), jnp.float32, low / len(cuts), largest / len(cuts))
        gain = gain * jnp.repeat(jnp.exp(heights), shape[dim] // blocks).reshape((-1,) + (1,) * (len(shape) - 1 - dim))
    return gain


def normal_values(own_key, dims, spread, most, split=(), kind=jnp.bfloat16):
    gain = shard_levels(own_key, dims, split, -0.22, 0.18) if split else 1.0
    array = jax.random.normal(own_key, dims, jnp.float32) * spread * gain
    return jnp.minimum(jnp.maximum(array, -most), most).astype(kind)


def setup_inputs(seed: int = 0) -> dict:
    streams_of = jax.random.split(jax.random.key(seed), 6)
    clip_in = normal_values(streams_of[0], (FRAMES, ROWS, C, COLS), 1.0, 6.0, ((0, 4), (1, 8)))
    kernel_one = normal_values(streams_of[1], (3, 3, 3, C, C), (27 * C) ** -0.5, 0.15625)
    bias_one = normal_values(streams_of[2], (C,), 0.5, 3.0, (), jnp.float32)
    kernel_two = normal_values(streams_of[3], (3, 3, 3, C, C), (27 * C // 4) ** -0.5, 0.3125)
    cotangent = normal_values(streams_of[4], (FRAMES, ROWS, C, COLS), 1.0, 6.0, ((0, 4), (1, 8)))
    return dict(clip_in=clip_in, kernel_one=kernel_one, bias_one=bias_one, kernel_two=kernel_two, cotangent=cotangent)


def conv(field, kernel):
    lhs = jnp.transpose(field.astype(jnp.float32), (2, 0, 1, 3))[None]
    rhs = jnp.transpose(kernel.astype(jnp.float32), (3, 4, 0, 1, 2))
    result = lax.conv_general_dilated(lhs, rhs, (1, 1, 1), [(2, 0), (1, 1), (1, 1)], dimension_numbers=('NCDHW', 'OIDHW', 'NCDHW'), precision=lax.Precision.HIGHEST)
    return jnp.transpose(result[0], (1, 2, 0, 3))

def reference(clip_in, kernel_one, bias_one, kernel_two, cotangent):
    hidden = conv(clip_in, kernel_one) + bias_one.astype(jnp.float32)[None, None, :, None]
    active = jax.nn.silu(hidden).astype(jnp.bfloat16)
    block_out = (clip_in.astype(jnp.float32) + conv(active, kernel_two)).astype(jnp.bfloat16)
    unused_two, pull_two = jax.vjp(conv, active.astype(jnp.float32), kernel_two.astype(jnp.float32))
    grad_act, grad_second = pull_two(cotangent.astype(jnp.float32))
    sig = jax.nn.sigmoid(hidden)
    grad_pre = (grad_act * sig * (1.0 + hidden * (1.0 - sig))).astype(jnp.bfloat16)
    unused_one, pull_one = jax.vjp(conv, clip_in.astype(jnp.float32), kernel_one.astype(jnp.float32))
    grad_back, grad_first = pull_one(grad_pre.astype(jnp.float32))
    grad_input = (cotangent.astype(jnp.float32) + grad_back).astype(jnp.bfloat16)
    inv_scale = 1.0 / math.sqrt(FRAMES * ROWS * COLS)
    grad_bias = lax.optimization_barrier(jnp.sum(grad_pre.astype(jnp.float32), axis=(0, 1, 3))) * inv_scale
    return (block_out, grad_input, grad_first * inv_scale, grad_second * inv_scale, grad_bias)
```

```python
import functools
import math

import jax
import jax.numpy as jnp
from jax import lax
from jax.experimental import pallas as pl
from jax.experimental.pallas import tpu as pltpu
from jax.sharding import PartitionSpec as P


def with_halo(block, sides, width):
    for axis, dim in sides:
        count = lax.axis_size(axis)
        forward = [(i, i + 1) for i in range(count - 1)]
        backward = [(target, source) for source, target in forward]
        low = lax.ppermute(
            lax.slice_in_dim(block, block.shape[dim] - width, None, axis=dim), axis, forward
        )
        high = lax.ppermute(lax.slice_in_dim(block, 0, width, axis=dim), axis, backward)
        block = jnp.concatenate([low, block, high], axis=dim)
    return block


def passed_along(value, axis, by):
    devices = lax.axis_size(axis)
    pairs = [(i, i + by) for i in range(devices) if 0 <= i + by < devices]
    return lax.ppermute(value, axis, pairs)


def extend_rows(field):
    return with_halo(field, (("rows", 1),), 1)


def with_prior(field):
    earlier = passed_along(field[-2:], "frames", 1)
    return jnp.concatenate([earlier, field], axis=0)


def with_later(field):
    following = passed_along(field[:2], "frames", -1)
    return jnp.concatenate([field, following], axis=0)


def spatial_taps(extended, row_count, col_count, flipped):
    padded = jnp.pad(extended, ((0, 0), (0, 0), (0, 0), (1, 1)))
    pieces = []
    for i in range(3):
        for j in range(3):
            row_start = 2 - i if flipped else i
            col_start = 2 - j if flipped else j
            pieces.append(
                padded[:, row_start : row_start + row_count, :, col_start : col_start + col_count]
            )
    return jnp.concatenate(pieces, axis=2)


def forward_conv(extended, kernel, frame_count, row_count, col_count):
    taps = spatial_taps(extended, row_count, col_count, False)
    chan_out = kernel.shape[3]
    running = None
    for t in range(3):
        flat_kernel = jnp.transpose(kernel[t], (2, 0, 1, 3)).reshape((chan_out, -1))
        term = jnp.einsum(
            "ok,frkw->frow",
            flat_kernel,
            taps[t : t + frame_count],
            preferred_element_type=jnp.float32,
        )
        running = term if running is None else running + term
    return running


def adjoint_conv(extended, kernel, frame_count, row_count, col_count):
    taps = spatial_taps(extended, row_count, col_count, True)
    chan_in = kernel.shape[4]
    running = None
    for t in range(3):
        flat_kernel = jnp.transpose(kernel[t], (3, 0, 1, 2)).reshape((chan_in, -1))
        term = jnp.einsum(
            "ck,frkw->frcw",
            flat_kernel,
            taps[2 - t : 2 - t + frame_count],
            preferred_element_type=jnp.float32,
        )
        running = term if running is None else running + term
    return running


def kernel_grad(upstream, extended):
    frame_count, row_count, chan_out, col_count = upstream.shape
    chan_in = extended.shape[2]
    taps = spatial_taps(extended, row_count, col_count, False)
    pieces = []
    for t in range(3):
        flat = jnp.einsum(
            "frow,frkw->ok", upstream, taps[t : t + frame_count], preferred_element_type=jnp.float32
        )
        pieces.append(jnp.transpose(flat.reshape((chan_out, 3, 3, chan_in)), (1, 2, 0, 3)))
    return jnp.stack(pieces, axis=0)


MESH = pl.DeviceIdType.MESH


def remote(src, dst, send_sem, recv_sem, device):
    return pltpu.make_async_remote_copy(
        src_ref=src,
        dst_ref=dst,
        send_sem=send_sem,
        recv_sem=recv_sem,
        device_id=device,
        device_id_type=MESH,
    )


def reduce_kernel(
    frames, rows, g_ref, out_ref, send, got_f, part, total, got_r, full,
    s_f, r_f, s_r, r_r, s_gr, r_gr, s_gf, r_gf,
):
    f, r = lax.axis_index("frames"), lax.axis_index("rows")
    chunk_f = g_ref.shape[0] // frames
    chunk_r = chunk_f // rows
    barrier = pltpu.get_barrier_semaphore()
    for d in range(1, frames):
        pl.semaphore_signal(
            barrier, inc=1, device_id=(lax.rem(f + d, frames), r), device_id_type=MESH
        )
    for d in range(1, rows):
        pl.semaphore_signal(
            barrier, inc=1, device_id=(f, lax.rem(r + d, rows)), device_id_type=MESH
        )
    pl.semaphore_wait(barrier, frames + rows - 2)

    send[...] = g_ref[...].astype(jnp.bfloat16)
    copies = []
    for d in range(1, frames):
        p = lax.rem(f + d, frames)
        at = pl.multiple_of(p * chunk_f, chunk_f)
        copies.append(
            remote(send.at[pl.ds(at, chunk_f)], got_f.at[d - 1], s_f.at[d - 1], r_f.at[d - 1], (p, r))
        )
        copies[-1].start()
    own_f = pl.multiple_of(f * chunk_f, chunk_f)
    total[...] = g_ref[pl.ds(own_f, chunk_f)]
    for d in range(1, frames):
        copies[d - 1].wait_recv()
        total[...] += got_f[d - 1].astype(jnp.float32)
    part[...] = total[...].astype(jnp.bfloat16)
    for d in range(1, rows):
        q = lax.rem(r + d, rows)
        at = pl.multiple_of(q * chunk_r, chunk_r)
        copies.append(
            remote(part.at[pl.ds(at, chunk_r)], got_r.at[d - 1], s_r.at[d - 1], r_r.at[d - 1], (f, q))
        )
        copies[-1].start()
    mine = total[pl.ds(pl.multiple_of(r * chunk_r, chunk_r), chunk_r)]
    for d in range(1, rows):
        copies[frames - 2 + d].wait_recv()
        mine = mine + got_r[d - 1].astype(jnp.float32)
    here = pl.ds(pl.multiple_of(f * chunk_f + r * chunk_r, chunk_r), chunk_r)
    full[here] = mine.astype(jnp.bfloat16)
    gathers = []
    for d in range(1, rows):
        gathers.append(
            remote(
                full.at[here], full.at[here], s_gr.at[d - 1], r_gr.at[d - 1],
                (f, lax.rem(r + d, rows)),
            )
        )
        gathers[-1].start()
    for copy in gathers:
        copy.wait_recv()
    block = pl.ds(own_f, chunk_f)
    for d in range(1, frames):
        gathers.append(
            remote(
                full.at[block], full.at[block], s_gf.at[d - 1], r_gf.at[d - 1],
                (lax.rem(f + d, frames), r),
            )
        )
        gathers[-1].start()
    for copy in gathers[rows - 1 :]:
        copy.wait_recv()
    out_ref[...] = full[...].astype(jnp.float32)
    for copy in copies + gathers:
        copy.wait_send()


def reduce_all(packed):
    frames, rows = lax.axis_size("frames"), lax.axis_size("rows")
    count = packed.shape[0]
    chunk_f = count // frames
    chunk_r = chunk_f // rows
    dma = pltpu.SemaphoreType.DMA
    return pl.pallas_call(
        functools.partial(reduce_kernel, frames, rows),
        out_shape=jax.ShapeDtypeStruct(packed.shape, jnp.float32),
        in_specs=[pl.BlockSpec(memory_space=pltpu.VMEM)],
        out_specs=pl.BlockSpec(memory_space=pltpu.VMEM),
        scratch_shapes=[
            pltpu.VMEM((count, 128), jnp.bfloat16),
            pltpu.VMEM((frames - 1, chunk_f, 128), jnp.bfloat16),
            pltpu.VMEM((chunk_f, 128), jnp.bfloat16),
            pltpu.VMEM((chunk_f, 128), jnp.float32),
            pltpu.VMEM((rows - 1, chunk_r, 128), jnp.bfloat16),
            pltpu.VMEM((count, 128), jnp.bfloat16),
            dma((frames - 1,)), dma((frames - 1,)),
            dma((rows - 1,)), dma((rows - 1,)),
            dma((rows - 1,)), dma((rows - 1,)),
            dma((frames - 1,)), dma((frames - 1,)),
        ],
        compiler_params=pltpu.CompilerParams(
            collective_id=0, has_side_effects=True, vmem_limit_bytes=32 * 1024 * 1024
        ),
    )(packed)


def per_device(clip_in, kernel_one, bias_one, kernel_two, cotangent):
    frame_count, row_count, channels, col_count = clip_in.shape
    input_rows = extend_rows(clip_in)
    cot_rows = None
    input_ext = with_prior(input_rows)
    hidden = (
        forward_conv(input_ext, kernel_one, frame_count, row_count, col_count)
        + bias_one[None, None, :, None]
    )
    active = jax.nn.silu(hidden).astype(jnp.bfloat16)
    active_ext = with_prior(extend_rows(active))
    block_out = (
        clip_in.astype(jnp.float32)
        + forward_conv(active_ext, kernel_two, frame_count, row_count, col_count)
    ).astype(jnp.bfloat16)
    cot_rows = extend_rows(cotangent)
    cot_ext = with_later(cot_rows)
    grad_act = adjoint_conv(cot_ext, kernel_two, frame_count, row_count, col_count)
    sig = jax.nn.sigmoid(hidden)
    grad_pre = (grad_act * sig * (1.0 + hidden * (1.0 - sig))).astype(jnp.bfloat16)
    pre_ext = with_later(extend_rows(grad_pre))
    grad_back = adjoint_conv(pre_ext, kernel_one, frame_count, row_count, col_count)
    grad_input = (cotangent.astype(jnp.float32) + grad_back).astype(jnp.bfloat16)
    term_second = kernel_grad(cotangent, active_ext)
    term_first = kernel_grad(grad_pre, input_ext)
    term_bias = jnp.sum(grad_pre.astype(jnp.float32), axis=(0, 1, 3))
    size = term_first.size
    step = lax.axis_size("frames") * lax.axis_size("rows") * 16 * 128
    flat = jnp.concatenate([term_first.reshape(-1), term_second.reshape(-1), term_bias])
    flat = jnp.pad(flat, (0, -flat.size % step))
    total = reduce_all(flat.reshape((-1, 128))).reshape(-1)
    total_first = total[:size].reshape(term_first.shape)
    total_second = total[size : 2 * size].reshape(term_second.shape)
    total_bias = total[2 * size : 2 * size + channels]
    cell_total = (
        frame_count * lax.axis_size("frames") * row_count * lax.axis_size("rows") * col_count
    )
    inv_scale = 1.0 / math.sqrt(cell_total)
    return (
        block_out,
        grad_input,
        total_first * inv_scale,
        total_second * inv_scale,
        total_bias * inv_scale,
    )


def solution(mesh):
    in_specs = (P("frames", "rows", None, None), P(), P(), P(), P("frames", "rows", None, None))
    out_specs = (P("frames", "rows", None, None), P("frames", "rows", None, None), P(), P(), P())
    return jax.shard_map(
        per_device, mesh=mesh, in_specs=in_specs, out_specs=out_specs, check_vma=False
    )
```

```python
import functools
import math

import jax
import jax.numpy as jnp
from jax import lax
from jax.experimental import pallas as pl
from jax.experimental.pallas import tpu as pltpu
from jax.sharding import PartitionSpec as P

MESH = pl.DeviceIdType.MESH
LANES = 128


def remote(src, dst, send_sem, recv_sem, device):
    return pltpu.make_async_remote_copy(
        src_ref=src,
        dst_ref=dst,
        send_sem=send_sem,
        recv_sem=recv_sem,
        device_id=device,
        device_id_type=MESH,
    )


class Halo:
    def __init__(self, field, sems, later, sizes, place):
        self.field, self.later = field, later
        frames, rows = sizes
        f, r = place
        self.frame_count, self.row_count = field.shape[0] - 2, field.shape[1] - 2
        chan = self.chan = field.shape[2] // 3
        fc, rc = self.frame_count, self.row_count
        mid = pl.ds(chan, chan)
        self.first = 0 if later else 2
        local = pl.ds(self.first, fc)
        edge, rim = (pl.ds(0, 2), pl.ds(fc, 2)) if later else (pl.ds(fc, 2), pl.ds(0, 2))
        self.rim_first = fc if later else 0
        up, down = lax.rem(r + 1, rows), lax.rem(r + rows - 1, rows)
        side = lax.rem(f + (frames - 1 if later else 1), frames)
        to_up, to_down = r < rows - 1, r > 0
        to_side, from_side = (f > 0, f < frames - 1) if later else (f < frames - 1, f > 0)
        self.items = []
        plan = [
            (local, rc, local, 0, (f, up), to_up, to_down),
            (local, 1, local, rc + 1, (f, down), to_down, to_up),
            (edge, pl.ds(1, rc), rim, pl.ds(1, rc), (side, r), to_side, from_side),
            (edge, rc, rim, 0, (side, up), to_side & to_up, from_side & to_down),
            (edge, 1, rim, rc + 1, (side, down), to_side & to_down, from_side & to_up),
        ]
        for n, (se, sr, de, dr, device, sends, gets) in enumerate(plan):
            target = field.at[de, dr, mid]
            copy = remote(field.at[se, sr, mid], target, sems.at[0, n], sems.at[1, n], device)
            self.items.append((copy, target, sends, gets))

    def start(self):
        for copy, _, sends, _ in self.items:
            pl.when(sends)(copy.start)

    def shift(self, first, count, rows):
        field, chan = self.field, self.chan

        def body(e, carry):
            for row in rows:
                value = field[e, row, chan : 2 * chan].astype(jnp.float32)
                cols = value.shape[1]
                lane = lax.broadcasted_iota(jnp.int32, value.shape, 1)
                left = jnp.where(lane == 0, 0.0, pltpu.roll(value, 1, 1))
                right = jnp.where(lane == cols - 1, 0.0, pltpu.roll(value, cols - 1, 1))
                field[e, row, 0:chan] = left.astype(jnp.bfloat16)
                field[e, row, 2 * chan : 3 * chan] = right.astype(jnp.bfloat16)
            return carry

        lax.fori_loop(first, first + count, body, 0)

    def shift_local(self):
        self.shift(self.first, self.frame_count, range(1, self.row_count + 1))

    def finish(self):
        for copy, target, _, gets in self.items:
            pl.when(gets)(copy.wait_recv)

            def clear(target=target):
                target[...] = jnp.zeros(target.shape, jnp.bfloat16)

            pl.when(jnp.logical_not(gets))(clear)
        self.shift(self.first, self.frame_count, (0, self.row_count + 1))
        self.shift(self.rim_first, 2, range(self.row_count + 2))

    def drain(self):
        for copy, _, sends, _ in self.items:
            pl.when(sends)(copy.wait_send)


def offsets(e, frame_count):
    return max(0, e - frame_count + 1), min(2, e)


def convolve(field, weights, emit):
    frame_count, row_count = field.shape[0] - 2, field.shape[1] - 2
    chan, cols = field.shape[2] // 3, field.shape[3]

    def body(r, carry):
        sums = [None] * frame_count
        for e in range(frame_count + 2):
            low, high = offsets(e, frame_count)
            taps = field[e, pl.ds(r, 3)].reshape((9 * chan, cols))
            part = jnp.dot(
                weights[low * chan : (high + 1) * chan], taps, preferred_element_type=jnp.float32
            )
            for t in range(low, high + 1):
                term = part[(t - low) * chan : (t - low + 1) * chan]
                sums[e - t] = term if sums[e - t] is None else sums[e - t] + term
        for f in range(frame_count):
            emit(f, r, sums[f])
        return carry

    lax.fori_loop(0, row_count, body, 0)


def kernel_grad(upstream, field, total):
    frame_count, row_count = field.shape[0] - 2, field.shape[1] - 2
    chan, cols = field.shape[2] // 3, field.shape[3]
    total[...] = jnp.zeros(total.shape, jnp.float32)

    def body(r, carry):
        for e in range(frame_count + 2):
            low, high = offsets(e, frame_count)
            taps = field[e, pl.ds(r, 3)].reshape((9 * chan, cols))
            left = jnp.concatenate(
                [upstream[e - t, r + 1, chan : 2 * chan] for t in range(low, high + 1)], axis=0
            )
            part = lax.dot_general(
                left, taps, (((1,), (1,)), ((), ())), preferred_element_type=jnp.float32
            )
            total[low * chan : (high + 1) * chan, 0 : 9 * chan] += part
        return carry

    lax.fori_loop(0, row_count, body, 0)


def block_kernel(
    frames, rows, inv_scale,
    clip_ref, cot_ref, one_ref, two_ref, one_adj_ref, two_adj_ref, bias_ref,
    block_ref, input_ref, first_ref, second_ref, bias_out_ref,
    clip_f, cot_f, act_f, pre_f, slope, first_sum, second_sum, bias_sum,
    send, got_f, part, total, got_r, full,
    halo_sems, sems_f, sems_r, sems_gr, sems_gf,
):
    f, r = lax.axis_index("frames"), lax.axis_index("rows")
    frame_count, row_count, chan, cols = clip_ref.shape
    place, sizes = (f, r), (frames, rows)

    barrier = pltpu.get_barrier_semaphore()
    others = [(lax.rem(f + d, frames), r) for d in range(1, frames)]
    others += [(f, lax.rem(r + d, rows)) for d in range(1, rows)]
    for df in (1, frames - 1):
        for dr in (1, rows - 1):
            others.append((lax.rem(f + df, frames), lax.rem(r + dr, rows)))
    for device in others:
        pl.semaphore_signal(barrier, inc=1, device_id=device, device_id_type=MESH)
    mid = slice(chan, 2 * chan)
    clip_f[2 : frame_count + 2, 1 : row_count + 1, mid] = clip_ref[...]
    cot_f[0:frame_count, 1 : row_count + 1, mid] = cot_ref[...]
    pl.semaphore_wait(barrier, len(others))

    clip_h = Halo(clip_f, halo_sems.at[0], False, sizes, place)
    cot_h = Halo(cot_f, halo_sems.at[1], True, sizes, place)
    act_h = Halo(act_f, halo_sems.at[2], False, sizes, place)
    pre_h = Halo(pre_f, halo_sems.at[3], True, sizes, place)
    clip_h.start()
    cot_h.start()
    clip_h.shift_local()
    cot_h.shift_local()
    clip_h.finish()

    def emit_hidden(fr, rr, value):
        hidden = value + bias_ref[...]
        sig = 1.0 / (1.0 + jnp.exp(-hidden))
        act_f[fr + 2, rr + 1, mid] = (hidden * sig).astype(jnp.bfloat16)
        slope[fr, rr] = sig * (1.0 + hidden * (1.0 - sig))

    convolve(clip_f, one_ref, emit_hidden)
    act_h.start()
    act_h.shift_local()

    cot_h.finish()
    bias_sum[...] = jnp.zeros(bias_sum.shape, jnp.float32)

    def emit_pre(fr, rr, value):
        pre = (value * slope[fr, rr]).astype(jnp.bfloat16)
        pre_f[fr, rr + 1, mid] = pre
        bias_sum[...] += pre.astype(jnp.float32)

    convolve(cot_f, two_adj_ref, emit_pre)
    pre_h.start()
    pre_h.shift_local()

    act_h.finish()
    kernel_grad(cot_f, act_f, second_sum)
    kernel_grad(pre_f, clip_f, first_sum)

    wide = second_sum.shape[1] // LANES
    tall = second_sum.shape[0]
    half = wide * tall + chan
    for k, grad in enumerate((first_sum, second_sum)):
        for b in range(wide):
            send[pl.ds(k * half + b * tall, tall)] = grad[:, b * LANES : (b + 1) * LANES].astype(
                jnp.bfloat16
            )
    bias_term = jnp.sum(bias_sum[...], axis=1, keepdims=True)
    bias_rows = jnp.broadcast_to(bias_term, (chan, LANES)).astype(jnp.bfloat16)
    send[pl.ds(half - chan, chan)] = bias_rows
    send[pl.ds(2 * half - chan, chan)] = bias_rows
    count = send.shape[0]
    if count > 2 * half:
        send[pl.ds(2 * half, count - 2 * half)] = jnp.zeros((count - 2 * half, LANES), jnp.bfloat16)
    chunk_f = count // frames
    chunk_r = chunk_f // rows
    copies = []
    for d in range(1, frames):
        p = lax.rem(f + d, frames)
        at = pl.multiple_of(p * chunk_f, chunk_f)
        copies.append(
            remote(
                send.at[pl.ds(at, chunk_f)], got_f.at[d - 1],
                sems_f.at[0, d - 1], sems_f.at[1, d - 1], (p, r),
            )
        )
        copies[-1].start()

    def emit_block(fr, rr, value):
        block_ref[fr, rr] = (clip_ref[fr, rr].astype(jnp.float32) + value).astype(jnp.bfloat16)

    convolve(act_f, two_ref, emit_block)

    own_f = pl.multiple_of(f * chunk_f, chunk_f)
    total[...] = send[pl.ds(own_f, chunk_f)].astype(jnp.float32)
    for d in range(1, frames):
        copies[d - 1].wait_recv()
        total[...] += got_f[d - 1].astype(jnp.float32)
    part[...] = total[...].astype(jnp.bfloat16)
    for d in range(1, rows):
        q = lax.rem(r + d, rows)
        at = pl.multiple_of(q * chunk_r, chunk_r)
        copies.append(
            remote(
                part.at[pl.ds(at, chunk_r)], got_r.at[d - 1],
                sems_r.at[0, d - 1], sems_r.at[1, d - 1], (f, q),
            )
        )
        copies[-1].start()

    pre_h.finish()

    def emit_input(fr, rr, value):
        input_ref[fr, rr] = (cot_ref[fr, rr].astype(jnp.float32) + value).astype(jnp.bfloat16)

    convolve(pre_f, one_adj_ref, emit_input)

    mine = total[pl.ds(pl.multiple_of(r * chunk_r, chunk_r), chunk_r)]
    for d in range(1, rows):
        copies[frames - 2 + d].wait_recv()
        mine = mine + got_r[d - 1].astype(jnp.float32)
    here = pl.ds(pl.multiple_of(f * chunk_f + r * chunk_r, chunk_r), chunk_r)
    full[here] = mine.astype(jnp.bfloat16)
    gathers = []
    for d in range(1, rows):
        gathers.append(
            remote(
                full.at[here], full.at[here], sems_gr.at[0, d - 1], sems_gr.at[1, d - 1],
                (f, lax.rem(r + d, rows)),
            )
        )
        gathers[-1].start()
    for copy in gathers:
        copy.wait_recv()
    block = pl.ds(own_f, chunk_f)
    for d in range(1, frames):
        gathers.append(
            remote(
                full.at[block], full.at[block], sems_gf.at[0, d - 1], sems_gf.at[1, d - 1],
                (lax.rem(f + d, frames), r),
            )
        )
        gathers[-1].start()
    for copy in gathers[rows - 1 :]:
        copy.wait_recv()

    for k, out in enumerate((first_ref, second_ref)):
        for t in range(3):
            for tap in range(9):
                lane = tap * chan
                b, inner = lane // LANES, lane % LANES
                tile = full[pl.ds(k * half + b * tall + t * chan, chan)]
                out[t, tap // 3, tap % 3] = (
                    tile[:, inner : inner + chan].astype(jnp.float32) * inv_scale
                )
    bias_out_ref[...] = full[pl.ds(half - chan, chan)].astype(jnp.float32) * inv_scale
    for copy in copies + gathers:
        copy.wait_send()
    for halo in (clip_h, cot_h, act_h, pre_h):
        halo.drain()


def per_device(clip_in, kernel_one, bias_one, kernel_two, cotangent):
    frame_count, row_count, chan, cols = clip_in.shape
    frames, rows = lax.axis_size("frames"), lax.axis_size("rows")
    inv_scale = 1.0 / math.sqrt(frame_count * frames * row_count * rows * cols)

    def forward(kernel):
        return jnp.transpose(kernel, (0, 3, 1, 2, 4)).reshape((3 * chan, 9 * chan))

    def adjoint(kernel):
        flipped = jnp.flip(kernel, (0, 1, 2))
        return jnp.transpose(flipped, (0, 4, 1, 2, 3)).reshape((3 * chan, 9 * chan))

    wide = -(-9 * chan // LANES)
    tall = 3 * chan
    count = 2 * (wide * tall + chan)
    count += -count % (frames * rows * 16)
    chunk_f = count // frames
    chunk_r = chunk_f // rows
    dma = pltpu.SemaphoreType.DMA
    bf16, f32 = jnp.bfloat16, jnp.float32
    field = pltpu.VMEM((frame_count + 2, row_count + 2, 3 * chan, cols), bf16)
    vmem = pl.BlockSpec(memory_space=pltpu.VMEM)
    block, grad_input, first, second, bias = pl.pallas_call(
        functools.partial(block_kernel, frames, rows, inv_scale),
        out_shape=(
            jax.ShapeDtypeStruct(clip_in.shape, bf16),
            jax.ShapeDtypeStruct(clip_in.shape, bf16),
            jax.ShapeDtypeStruct(kernel_one.shape, f32),
            jax.ShapeDtypeStruct(kernel_two.shape, f32),
            jax.ShapeDtypeStruct((chan, LANES), f32),
        ),
        in_specs=[vmem] * 7,
        out_specs=(vmem,) * 5,
        scratch_shapes=[
            field, field, field, field,
            pltpu.VMEM(clip_in.shape, f32),
            pltpu.VMEM((tall, wide * LANES), f32),
            pltpu.VMEM((tall, wide * LANES), f32),
            pltpu.VMEM((chan, cols), f32),
            pltpu.VMEM((count, LANES), bf16),
            pltpu.VMEM((frames - 1, chunk_f, LANES), bf16),
            pltpu.VMEM((chunk_f, LANES), bf16),
            pltpu.VMEM((chunk_f, LANES), f32),
            pltpu.VMEM((rows - 1, chunk_r, LANES), bf16),
            pltpu.VMEM((count, LANES), bf16),
            dma((4, 2, 5)),
            dma((2, frames - 1)),
            dma((2, rows - 1)),
            dma((2, rows - 1)),
            dma((2, frames - 1)),
        ],
        compiler_params=pltpu.CompilerParams(
            collective_id=0, has_side_effects=True, vmem_limit_bytes=48 * 1024 * 1024
        ),
    )(
        clip_in, cotangent, forward(kernel_one), forward(kernel_two),
        adjoint(kernel_one), adjoint(kernel_two), bias_one.reshape((chan, 1)),
    )
    return block, grad_input, first, second, bias[:, 0]


def solution(mesh):
    in_specs = (P("frames", "rows", None, None), P(), P(), P(), P("frames", "rows", None, None))
    out_specs = (P("frames", "rows", None, None), P("frames", "rows", None, None), P(), P(), P())
    return jax.shard_map(
        per_device, mesh=mesh, in_specs=in_specs, out_specs=out_specs, check_vma=False
    )
```

```python
import functools
import math

import jax
import jax.numpy as jnp
from jax import lax
from jax.experimental import pallas as pl
from jax.experimental.pallas import tpu as pltpu
from jax.sharding import PartitionSpec as P

MESH = pl.DeviceIdType.MESH
LANES = 128


def remote(src, dst, send_sem, recv_sem, device):
    return pltpu.make_async_remote_copy(
        src_ref=src,
        dst_ref=dst,
        send_sem=send_sem,
        recv_sem=recv_sem,
        device_id=device,
        device_id_type=MESH,
    )


class Halo:
    def __init__(self, field, sems, later, sizes, place):
        self.field, self.later = field, later
        frames, rows = sizes
        f, r = place
        self.frame_count, self.row_count = field.shape[0] - 2, field.shape[1] - 2
        chan = self.chan = field.shape[2] // 3
        fc, rc = self.frame_count, self.row_count
        mid = pl.ds(chan, chan)
        self.first = 0 if later else 2
        local = pl.ds(self.first, fc)
        edge, rim = (pl.ds(0, 2), pl.ds(fc, 2)) if later else (pl.ds(fc, 2), pl.ds(0, 2))
        self.rim_first = fc if later else 0
        up, down = lax.rem(r + 1, rows), lax.rem(r + rows - 1, rows)
        side = lax.rem(f + (frames - 1 if later else 1), frames)
        to_up, to_down = r < rows - 1, r > 0
        to_side, from_side = (f > 0, f < frames - 1) if later else (f < frames - 1, f > 0)
        self.items = []
        plan = [
            (local, rc, local, 0, (f, up), to_up, to_down),
            (local, 1, local, rc + 1, (f, down), to_down, to_up),
            (edge, pl.ds(1, rc), rim, pl.ds(1, rc), (side, r), to_side, from_side),
            (edge, rc, rim, 0, (side, up), to_side & to_up, from_side & to_down),
            (edge, 1, rim, rc + 1, (side, down), to_side & to_down, from_side & to_up),
        ]
        for n, (se, sr, de, dr, device, sends, gets) in enumerate(plan):
            target = field.at[de, dr, mid]
            copy = remote(field.at[se, sr, mid], target, sems.at[0, n], sems.at[1, n], device)
            self.items.append((copy, target, sends, gets))

    def start(self):
        for copy, _, sends, _ in self.items:
            pl.when(sends)(copy.start)

    def shift(self, first, count, rows):
        field, chan = self.field, self.chan

        def body(e, carry):
            for row in rows:
                value = field[e, row, chan : 2 * chan].astype(jnp.float32)
                cols = value.shape[1]
                lane = lax.broadcasted_iota(jnp.int32, value.shape, 1)
                left = jnp.where(lane == 0, 0.0, pltpu.roll(value, 1, 1))
                right = jnp.where(lane == cols - 1, 0.0, pltpu.roll(value, cols - 1, 1))
                field[e, row, 0:chan] = left.astype(jnp.bfloat16)
                field[e, row, 2 * chan : 3 * chan] = right.astype(jnp.bfloat16)
            return carry

        lax.fori_loop(first, first + count, body, 0)

    def shift_local(self):
        self.shift(self.first, self.frame_count, range(1, self.row_count + 1))

    def receive(self):
        for copy, target, _, gets in self.items:
            pl.when(gets)(copy.wait_recv)

            def clear(target=target):
                target[...] = jnp.zeros(target.shape, jnp.bfloat16)

            pl.when(jnp.logical_not(gets))(clear)

    def shift_rim(self):
        self.shift(self.first, self.frame_count, (0, self.row_count + 1))
        self.shift(self.rim_first, 2, range(self.row_count + 2))

    def drain(self):
        for copy, _, sends, _ in self.items:
            pl.when(sends)(copy.wait_send)


def offsets(e, frame_count):
    return max(0, e - frame_count + 1), min(2, e)


def convolve(field, weights, emit, start=0, stop=None):
    frame_count, row_count = field.shape[0] - 2, field.shape[1] - 2
    chan, cols = field.shape[2] // 3, field.shape[3]

    def body(r, carry):
        sums = [None] * frame_count
        for e in range(frame_count + 2):
            low, high = offsets(e, frame_count)
            taps = field[e, pl.ds(r, 3)].reshape((9 * chan, cols))
            part = jnp.dot(
                weights[low * chan : (high + 1) * chan, 0 : 9 * chan],
                taps,
                preferred_element_type=jnp.float32,
            )
            for t in range(low, high + 1):
                term = part[(t - low) * chan : (t - low + 1) * chan]
                sums[e - t] = term if sums[e - t] is None else sums[e - t] + term
        for f in range(frame_count):
            emit(f, r, sums[f])
        return carry

    lax.fori_loop(start, row_count if stop is None else stop, body, 0)


def kernel_grad(upstream, field, total):
    frame_count, row_count = field.shape[0] - 2, field.shape[1] - 2
    chan, cols = field.shape[2] // 3, field.shape[3]
    total[...] = jnp.zeros(total.shape, jnp.float32)
    blank = jnp.zeros((chan, row_count * cols), jnp.bfloat16)
    for e in range(frame_count + 2):
        low, high = offsets(e, frame_count)
        taps = jnp.concatenate(
            [field[e, r : r + 3].reshape((9 * chan, cols)) for r in range(row_count)], axis=1
        )
        right = []
        for t in range(3):
            if low <= t <= high:
                lines = [upstream[e - t, r + 1, chan : 2 * chan] for r in range(row_count)]
                right.append(jnp.concatenate(lines, axis=1))
            else:
                right.append(blank)
        total[0 : 9 * chan, 0 : 3 * chan] += lax.dot_general(
            taps,
            jnp.concatenate(right, axis=0),
            (((1,), (1,)), ((), ())),
            preferred_element_type=jnp.float32,
        )


def lay_forward(kernel, weights):
    chan = kernel.shape[3]
    for t in range(3):
        for tap in range(9):
            weights[t * chan : (t + 1) * chan, tap * chan : (tap + 1) * chan] = kernel[
                t, tap // 3, tap % 3
            ]


def lay_adjoint(kernel, weights):
    chan = kernel.shape[3]
    for t in range(3):
        for tap in range(9):
            piece = kernel[2 - t, 2 - tap // 3, 2 - tap % 3].astype(jnp.float32)
            weights[t * chan : (t + 1) * chan, tap * chan : (tap + 1) * chan] = jnp.transpose(
                piece
            ).astype(jnp.bfloat16)


class Reduction:
    def __init__(self, bufs, sems, sizes, place):
        self.send, self.got_f, self.part, self.total, self.got_r, self.full = bufs
        self.sems = sems
        self.sizes, self.place = sizes, place
        frames, rows = sizes
        f, r = place
        self.chunk_f = self.send.shape[0] // frames
        self.chunk_r = self.chunk_f // rows
        self.own_f = pl.multiple_of(f * self.chunk_f, self.chunk_f)
        self.frame_peers = [lax.rem(f + d, frames) for d in range(1, frames)]
        self.row_peers = [lax.rem(r + d, rows) for d in range(1, rows)]

    def copy(self, src, dst, kind, n, device):
        return remote(src, dst, self.sems.at[kind, 0, n], self.sems.at[kind, 1, n], device)

    def scatter_frames(self):
        _, r = self.place
        self.first = []
        for n, p in enumerate(self.frame_peers):
            at = pl.ds(pl.multiple_of(p * self.chunk_f, self.chunk_f), self.chunk_f)
            self.first.append(self.copy(self.send.at[at], self.got_f.at[n], 0, n, (p, r)))
            self.first[-1].start()

    def scatter_rows(self):
        f, _ = self.place
        value = self.send[pl.ds(self.own_f, self.chunk_f)].astype(jnp.float32)
        for n, copy in enumerate(self.first):
            copy.wait_recv()
            value = value + self.got_f[n].astype(jnp.float32)
        self.total[...] = value
        self.part[...] = value.astype(jnp.bfloat16)
        self.second = []
        for n, q in enumerate(self.row_peers):
            at = pl.ds(pl.multiple_of(q * self.chunk_r, self.chunk_r), self.chunk_r)
            self.second.append(self.copy(self.part.at[at], self.got_r.at[n], 1, n, (f, q)))
            self.second[-1].start()

    def gather_rows(self):
        f, r = self.place
        own = pl.multiple_of(r * self.chunk_r, self.chunk_r)
        value = self.total[pl.ds(own, self.chunk_r)]
        for n, copy in enumerate(self.second):
            copy.wait_recv()
            value = value + self.got_r[n].astype(jnp.float32)
        at = pl.multiple_of(f * self.chunk_f + r * self.chunk_r, self.chunk_r)
        here = self.full.at[pl.ds(at, self.chunk_r)]
        here[...] = value.astype(jnp.bfloat16)
        self.third = []
        for n, q in enumerate(self.row_peers):
            self.third.append(self.copy(here, here, 2, n, (f, q)))
            self.third[-1].start()

    def gather_frames(self):
        _, r = self.place
        for copy in self.third:
            copy.wait_recv()
        block = self.full.at[pl.ds(self.own_f, self.chunk_f)]
        self.fourth = []
        for n, p in enumerate(self.frame_peers):
            self.fourth.append(self.copy(block, block, 3, n, (p, r)))
            self.fourth[-1].start()

    def finish(self):
        for copy in self.fourth:
            copy.wait_recv()

    def drain(self):
        for copy in self.first + self.second + self.third + self.fourth:
            copy.wait_send()


def block_kernel(
    frames, rows, inv_scale,
    clip_ref, cot_ref, one_ref, two_ref, bias_ref,
    block_ref, input_ref, first_ref, second_ref, bias_out_ref,
    clip_f, cot_f, act_f, pre_f, slope, one_w, two_w, one_adj, two_adj, grad_sum, bias_sum,
    send, got_f, part, total, got_r, full,
    halo_sems, reduce_sems,
):
    f, r = lax.axis_index("frames"), lax.axis_index("rows")
    frame_count, row_count, chan, cols = clip_ref.shape
    place, sizes = (f, r), (frames, rows)

    barrier = pltpu.get_barrier_semaphore()
    others = [(lax.rem(f + d, frames), r) for d in range(1, frames)]
    others += [(f, lax.rem(r + d, rows)) for d in range(1, rows)]
    for df in (1, frames - 1):
        for dr in (1, rows - 1):
            others.append((lax.rem(f + df, frames), lax.rem(r + dr, rows)))
    for device in others:
        pl.semaphore_signal(barrier, inc=1, device_id=device, device_id_type=MESH)
    mid = slice(chan, 2 * chan)
    clip_f[2 : frame_count + 2, 1 : row_count + 1, mid] = clip_ref[...]
    cot_f[0:frame_count, 1 : row_count + 1, mid] = cot_ref[...]
    pl.semaphore_wait(barrier, len(others))

    clip_h = Halo(clip_f, halo_sems.at[0], False, sizes, place)
    cot_h = Halo(cot_f, halo_sems.at[1], True, sizes, place)
    act_h = Halo(act_f, halo_sems.at[2], False, sizes, place)
    pre_h = Halo(pre_f, halo_sems.at[3], True, sizes, place)
    clip_h.start()
    lay_forward(one_ref, one_w)
    clip_h.shift_local()
    lay_adjoint(two_ref, two_adj)
    clip_h.receive()
    cot_h.start()
    clip_h.shift_rim()

    def emit_hidden(fr, rr, value):
        hidden = value + bias_ref[...]
        sig = 1.0 / (1.0 + jnp.exp(-hidden))
        act_f[fr + 2, rr + 1, mid] = (hidden * sig).astype(jnp.bfloat16)
        slope[fr, rr] = sig * (1.0 + hidden * (1.0 - sig))

    convolve(clip_f, one_w, emit_hidden)
    act_h.start()
    cot_h.shift_local()
    act_h.shift_local()

    cot_h.receive()
    cot_h.shift_rim()
    bias_sum[...] = jnp.zeros(bias_sum.shape, jnp.float32)

    def emit_pre(fr, rr, value):
        pre = (value * slope[fr, rr]).astype(jnp.bfloat16)
        pre_f[fr, rr + 1, mid] = pre
        bias_sum[...] += pre.astype(jnp.float32)

    convolve(cot_f, two_adj, emit_pre)
    pre_h.start()

    wide = one_w.shape[1] // LANES
    tall = one_w.shape[0]
    used = wide * tall + chan
    reductions = [
        Reduction(
            [buf.at[k] for buf in (send, got_f, part, total, got_r, full)],
            reduce_sems.at[k], sizes, place,
        )
        for k in range(2)
    ]
    bias_term = jnp.sum(bias_sum[...], axis=1, keepdims=True)
    bias_rows = jnp.broadcast_to(bias_term, (chan, LANES)).astype(jnp.bfloat16)
    rest = send.shape[1] - used

    def reduce_grad(k):
        flipped = jnp.transpose(grad_sum[...])
        for b in range(wide):
            send[k, pl.ds(b * tall, tall)] = flipped[:tall, b * LANES : (b + 1) * LANES].astype(
                jnp.bfloat16
            )
        send[k, pl.ds(used - chan, chan)] = bias_rows
        if rest:
            send[k, pl.ds(used, rest)] = jnp.zeros((rest, LANES), jnp.bfloat16)
        reductions[k].scatter_frames()

    kernel_grad(pre_f, clip_f, grad_sum)
    reduce_grad(0)
    act_h.receive()
    act_h.shift_rim()
    kernel_grad(cot_f, act_f, grad_sum)
    reduce_grad(1)
    lay_forward(two_ref, two_w)
    lay_adjoint(one_ref, one_adj)
    pre_h.shift_local()

    def emit_block(fr, rr, value):
        block_ref[fr, rr] = (clip_ref[fr, rr].astype(jnp.float32) + value).astype(jnp.bfloat16)

    half_way = row_count // 2
    convolve(act_f, two_w, emit_block, 0, half_way)
    reductions[0].scatter_rows()
    convolve(act_f, two_w, emit_block, half_way, row_count)
    reductions[1].scatter_rows()

    pre_h.receive()
    pre_h.shift_rim()

    def emit_input(fr, rr, value):
        input_ref[fr, rr] = (cot_ref[fr, rr].astype(jnp.float32) + value).astype(jnp.bfloat16)

    convolve(pre_f, one_adj, emit_input, 0, 1)
    reductions[0].gather_rows()
    reductions[1].gather_rows()
    convolve(pre_f, one_adj, emit_input, 1, half_way)
    reductions[0].gather_frames()
    reductions[1].gather_frames()
    convolve(pre_f, one_adj, emit_input, half_way, row_count)

    for k, out in enumerate((first_ref, second_ref)):
        reductions[k].finish()
        for t in range(3):
            for tap in range(9):
                lane = tap * chan
                b, inner = lane // LANES, lane % LANES
                tile = full[k, pl.ds(b * tall + t * chan, chan)]
                out[t, tap // 3, tap % 3] = (
                    tile[:, inner : inner + chan].astype(jnp.float32) * inv_scale
                )
    bias_out_ref[...] = full[0, pl.ds(used - chan, chan)].astype(jnp.float32) * inv_scale
    for reduction in reductions:
        reduction.drain()
    for halo in (clip_h, cot_h, act_h, pre_h):
        halo.drain()


def per_device(clip_in, kernel_one, bias_one, kernel_two, cotangent):
    frame_count, row_count, chan, cols = clip_in.shape
    frames, rows = lax.axis_size("frames"), lax.axis_size("rows")
    inv_scale = 1.0 / math.sqrt(frame_count * frames * row_count * rows * cols)

    wide = -(-9 * chan // LANES)
    tall = 3 * chan
    count = wide * tall + chan
    count += -count % (frames * rows * 16)
    chunk_f = count // frames
    chunk_r = chunk_f // rows
    dma = pltpu.SemaphoreType.DMA
    bf16, f32 = jnp.bfloat16, jnp.float32
    field = pltpu.VMEM((frame_count + 2, row_count + 2, 3 * chan, cols), bf16)
    weights = pltpu.VMEM((tall, wide * LANES), bf16)
    vmem = pl.BlockSpec(memory_space=pltpu.VMEM)
    block, grad_input, first, second, bias = pl.pallas_call(
        functools.partial(block_kernel, frames, rows, inv_scale),
        out_shape=(
            jax.ShapeDtypeStruct(clip_in.shape, bf16),
            jax.ShapeDtypeStruct(clip_in.shape, bf16),
            jax.ShapeDtypeStruct(kernel_one.shape, f32),
            jax.ShapeDtypeStruct(kernel_two.shape, f32),
            jax.ShapeDtypeStruct((chan, LANES), f32),
        ),
        in_specs=[vmem] * 5,
        out_specs=(vmem,) * 5,
        scratch_shapes=[
            field, field, field, field,
            pltpu.VMEM(clip_in.shape, f32),
            weights, weights, weights, weights,
            pltpu.VMEM((wide * LANES, -(-tall // LANES) * LANES), f32),
            pltpu.VMEM((chan, cols), f32),
            pltpu.VMEM((2, count, LANES), bf16),
            pltpu.VMEM((2, frames - 1, chunk_f, LANES), bf16),
            pltpu.VMEM((2, chunk_f, LANES), bf16),
            pltpu.VMEM((2, chunk_f, LANES), f32),
            pltpu.VMEM((2, rows - 1, chunk_r, LANES), bf16),
            pltpu.VMEM((2, count, LANES), bf16),
            dma((4, 2, 5)),
            dma((2, 4, 2, max(frames, rows) - 1)),
        ],
        compiler_params=pltpu.CompilerParams(
            collective_id=0, has_side_effects=True, vmem_limit_bytes=48 * 1024 * 1024
        ),
    )(
        clip_in, cotangent, kernel_one, kernel_two, bias_one.reshape((chan, 1)),
    )
    return block, grad_input, first, second, bias[:, 0]


def solution(mesh):
    in_specs = (P("frames", "rows", None, None), P(), P(), P(), P("frames", "rows", None, None))
    out_specs = (P("frames", "rows", None, None), P("frames", "rows", None, None), P(), P(), P())
    return jax.shard_map(
        per_device, mesh=mesh, in_specs=in_specs, out_specs=out_specs, check_vma=False
    )
```

```python
import functools
import math

import jax
import jax.numpy as jnp
from jax import lax
from jax.experimental import pallas as pl
from jax.experimental.pallas import tpu as pltpu
from jax.sharding import PartitionSpec as P

MESH = pl.DeviceIdType.MESH
LANES = 128


def remote(src, dst, send_sem, recv_sem, device):
    return pltpu.make_async_remote_copy(
        src_ref=src,
        dst_ref=dst,
        send_sem=send_sem,
        recv_sem=recv_sem,
        device_id=device,
        device_id_type=MESH,
    )


class Halo:
    def __init__(self, field, sems, later, sizes, place):
        self.field, self.later = field, later
        frames, rows = sizes
        f, r = place
        self.frame_count, self.row_count = field.shape[0] - 2, field.shape[1] - 2
        chan = self.chan = field.shape[2] // 3
        fc, rc = self.frame_count, self.row_count
        mid = pl.ds(chan, chan)
        self.first = 0 if later else 2
        local = pl.ds(self.first, fc)
        edge, rim = (pl.ds(0, 2), pl.ds(fc, 2)) if later else (pl.ds(fc, 2), pl.ds(0, 2))
        self.rim_first = fc if later else 0
        up, down = lax.rem(r + 1, rows), lax.rem(r + rows - 1, rows)
        side = lax.rem(f + (frames - 1 if later else 1), frames)
        to_up, to_down = r < rows - 1, r > 0
        to_side, from_side = (f > 0, f < frames - 1) if later else (f < frames - 1, f > 0)
        self.items = []
        plan = [
            (local, rc, local, 0, (f, up), to_up, to_down),
            (local, 1, local, rc + 1, (f, down), to_down, to_up),
            (edge, pl.ds(1, rc), rim, pl.ds(1, rc), (side, r), to_side, from_side),
            (edge, rc, rim, 0, (side, up), to_side & to_up, from_side & to_down),
            (edge, 1, rim, rc + 1, (side, down), to_side & to_down, from_side & to_up),
        ]
        for n, (se, sr, de, dr, device, sends, gets) in enumerate(plan):
            target = field.at[de, dr, mid]
            copy = remote(field.at[se, sr, mid], target, sems.at[0, n], sems.at[1, n], device)
            self.items.append((copy, target, sends, gets))

    def start(self):
        for copy, _, sends, _ in self.items:
            pl.when(sends)(copy.start)

    def shift(self, first, count, rows):
        field, chan = self.field, self.chan

        def body(e, carry):
            for row in rows:
                value = field[e, row, chan : 2 * chan].astype(jnp.float32)
                cols = value.shape[1]
                lane = lax.broadcasted_iota(jnp.int32, value.shape, 1)
                left = jnp.where(lane == 0, 0.0, pltpu.roll(value, 1, 1))
                right = jnp.where(lane == cols - 1, 0.0, pltpu.roll(value, cols - 1, 1))
                field[e, row, 0:chan] = left.astype(jnp.bfloat16)
                field[e, row, 2 * chan : 3 * chan] = right.astype(jnp.bfloat16)
            return carry

        lax.fori_loop(first, first + count, body, 0)

    def shift_local(self):
        self.shift(self.first, self.frame_count, range(1, self.row_count + 1))

    def receive(self):
        for copy, target, _, gets in self.items:
            pl.when(gets)(copy.wait_recv)

            def clear(target=target):
                target[...] = jnp.zeros(target.shape, jnp.bfloat16)

            pl.when(jnp.logical_not(gets))(clear)

    def shift_rim(self):
        self.shift(self.first, self.frame_count, (0, self.row_count + 1))
        self.shift(self.rim_first, 2, range(self.row_count + 2))

    def drain(self):
        for copy, _, sends, _ in self.items:
            pl.when(sends)(copy.wait_send)


def offsets(e, frame_count):
    return max(0, e - frame_count + 1), min(2, e)


def convolve(field, weights, emit, rows, frames=None, base=None):
    frame_count = field.shape[0] - 2
    chan, cols = field.shape[2] // 3, field.shape[3]
    start, count, step = rows

    def body(k, carry):
        r = start + k * step
        sums = [None if base is None else base[f, r] for f in range(frame_count)]
        for e in range(frame_count + 2) if frames is None else frames:
            low, high = offsets(e, frame_count)
            taps = field[e, pl.ds(r, 3)].reshape((9 * chan, cols))
            part = jnp.dot(
                weights[low * chan : (high + 1) * chan, 0 : 9 * chan],
                taps,
                preferred_element_type=jnp.float32,
            )
            for t in range(low, high + 1):
                term = part[(t - low) * chan : (t - low + 1) * chan]
                sums[e - t] = term if sums[e - t] is None else sums[e - t] + term
        for f in range(frame_count):
            emit(f, r, sums[f])
        return carry

    lax.fori_loop(0, count, body, 0)


def convolve_local(field, weights, first, partial):
    frame_count, row_count = field.shape[0] - 2, field.shape[1] - 2

    def keep(f, r, value):
        partial[f, r] = value

    convolve(
        field, weights, keep, (1, row_count - 2, 1), range(first, first + frame_count)
    )


def convolve_rest(field, weights, first, partial, emit):
    frame_count, row_count = field.shape[0] - 2, field.shape[1] - 2
    rim = [e for e in range(frame_count + 2) if not first <= e < first + frame_count]
    convolve(field, weights, emit, (1, row_count - 2, 1), rim, partial)
    convolve(field, weights, emit, (0, 2, row_count - 1))


def kernel_grad(upstream, field, total):
    frame_count, row_count = field.shape[0] - 2, field.shape[1] - 2
    chan, cols = field.shape[2] // 3, field.shape[3]
    total[...] = jnp.zeros(total.shape, jnp.float32)
    blank = jnp.zeros((chan, row_count * cols), jnp.bfloat16)
    for e in range(frame_count + 2):
        low, high = offsets(e, frame_count)
        taps = jnp.concatenate(
            [field[e, r : r + 3].reshape((9 * chan, cols)) for r in range(row_count)], axis=1
        )
        right = []
        for t in range(3):
            if low <= t <= high:
                lines = [upstream[e - t, r + 1, chan : 2 * chan] for r in range(row_count)]
                right.append(jnp.concatenate(lines, axis=1))
            else:
                right.append(blank)
        total[0 : 9 * chan, 0 : 3 * chan] += lax.dot_general(
            taps,
            jnp.concatenate(right, axis=0),
            (((1,), (1,)), ((), ())),
            preferred_element_type=jnp.float32,
        )


def lay_forward(kernel, weights):
    chan = kernel.shape[3]
    for t in range(3):
        for tap in range(9):
            weights[t * chan : (t + 1) * chan, tap * chan : (tap + 1) * chan] = kernel[
                t, tap // 3, tap % 3
            ]


def lay_adjoint(kernel, weights):
    chan = kernel.shape[3]
    for t in range(3):
        for tap in range(9):
            piece = kernel[2 - t, 2 - tap // 3, 2 - tap % 3].astype(jnp.float32)
            weights[t * chan : (t + 1) * chan, tap * chan : (tap + 1) * chan] = jnp.transpose(
                piece
            ).astype(jnp.bfloat16)


class Reduction:
    def __init__(self, bufs, sems, sizes, place):
        self.send, self.got_f, self.part, self.total, self.got_r, self.full = bufs
        self.sems = sems
        self.sizes, self.place = sizes, place
        frames, rows = sizes
        f, r = place
        self.chunk_f = self.send.shape[0] // frames
        self.chunk_r = self.chunk_f // rows
        self.own_f = pl.multiple_of(f * self.chunk_f, self.chunk_f)
        self.frame_peers = [lax.rem(f + d, frames) for d in range(1, frames)]
        self.row_peers = [lax.rem(r + d, rows) for d in range(1, rows)]

    def copy(self, src, dst, kind, n, device):
        return remote(src, dst, self.sems.at[kind, 0, n], self.sems.at[kind, 1, n], device)

    def scatter_frames(self):
        _, r = self.place
        self.first = []
        for n, p in enumerate(self.frame_peers):
            at = pl.ds(pl.multiple_of(p * self.chunk_f, self.chunk_f), self.chunk_f)
            self.first.append(self.copy(self.send.at[at], self.got_f.at[n], 0, n, (p, r)))
            self.first[-1].start()

    def scatter_rows(self):
        f, _ = self.place
        value = self.send[pl.ds(self.own_f, self.chunk_f)].astype(jnp.float32)
        for n, copy in enumerate(self.first):
            copy.wait_recv()
            value = value + self.got_f[n].astype(jnp.float32)
        self.total[...] = value
        self.part[...] = value.astype(jnp.bfloat16)
        self.second = []
        for n, q in enumerate(self.row_peers):
            at = pl.ds(pl.multiple_of(q * self.chunk_r, self.chunk_r), self.chunk_r)
            self.second.append(self.copy(self.part.at[at], self.got_r.at[n], 1, n, (f, q)))
            self.second[-1].start()

    def gather_rows(self):
        f, r = self.place
        own = pl.multiple_of(r * self.chunk_r, self.chunk_r)
        value = self.total[pl.ds(own, self.chunk_r)]
        for n, copy in enumerate(self.second):
            copy.wait_recv()
            value = value + self.got_r[n].astype(jnp.float32)
        at = pl.multiple_of(f * self.chunk_f + r * self.chunk_r, self.chunk_r)
        here = self.full.at[pl.ds(at, self.chunk_r)]
        here[...] = value.astype(jnp.bfloat16)
        self.third = []
        for n, q in enumerate(self.row_peers):
            self.third.append(self.copy(here, here, 2, n, (f, q)))
            self.third[-1].start()

    def gather_frames(self):
        _, r = self.place
        for copy in self.third:
            copy.wait_recv()
        block = self.full.at[pl.ds(self.own_f, self.chunk_f)]
        self.fourth = []
        for n, p in enumerate(self.frame_peers):
            self.fourth.append(self.copy(block, block, 3, n, (p, r)))
            self.fourth[-1].start()

    def finish(self):
        for copy in self.fourth:
            copy.wait_recv()

    def drain(self):
        for copy in self.first + self.second + self.third + self.fourth:
            copy.wait_send()


def block_kernel(
    frames, rows, inv_scale,
    clip_hbm, cot_hbm, one_hbm, two_hbm, bias_hbm,
    block_hbm, input_hbm, first_hbm, second_hbm, bias_out_ref,
    block_ref, input_ref, first_ref, second_ref, out_sems,
    one_ref, two_ref, bias_ref, local_sems,
    clip_f, cot_f, act_f, pre_f, slope, grad_act, one_w, two_w, one_adj, two_adj, grad_sum, bias_sum,
    send, got_f, part, total, got_r, full,
    halo_sems, reduce_sems,
):
    f, r = lax.axis_index("frames"), lax.axis_index("rows")
    frame_count, row_count, chan, cols = clip_hbm.shape
    place, sizes = (f, r), (frames, rows)

    mid = slice(chan, 2 * chan)
    inner = pl.ds(1, row_count), pl.ds(chan, chan)
    loads = [
        pltpu.make_async_copy(src, dst, local_sems.at[n])
        for n, (src, dst) in enumerate(
            (
                (clip_hbm, clip_f.at[pl.ds(2, frame_count), *inner]),
                (one_hbm, one_ref),
                (bias_hbm, bias_ref),
                (cot_hbm, cot_f.at[pl.ds(0, frame_count), *inner]),
                (two_hbm, two_ref),
            )
        )
    ]
    for load in loads:
        load.start()
    stores = [
        pltpu.make_async_copy(src, dst, out_sems.at[n])
        for n, (src, dst) in enumerate(
            (
                (block_ref, block_hbm),
                (input_ref, input_hbm),
                (first_ref, first_hbm),
                (second_ref, second_hbm),
            )
        )
    ]
    barrier = pltpu.get_barrier_semaphore()
    others = [(lax.rem(f + d, frames), r) for d in range(1, frames)]
    others += [(f, lax.rem(r + d, rows)) for d in range(1, rows)]
    for df in (1, frames - 1):
        for dr in (1, rows - 1):
            others.append((lax.rem(f + df, frames), lax.rem(r + dr, rows)))
    for device in others:
        pl.semaphore_signal(barrier, inc=1, device_id=device, device_id_type=MESH)
    loads[0].wait()
    pl.semaphore_wait(barrier, len(others))

    clip_h = Halo(clip_f, halo_sems.at[0], False, sizes, place)
    cot_h = Halo(cot_f, halo_sems.at[1], True, sizes, place)
    act_h = Halo(act_f, halo_sems.at[2], False, sizes, place)
    pre_h = Halo(pre_f, halo_sems.at[3], True, sizes, place)
    clip_h.start()
    loads[1].wait()
    lay_forward(one_ref, one_w)
    clip_h.shift_local()
    convolve_local(clip_f, one_w, 2, slope)
    for load in loads[2:]:
        load.wait()
    cot_h.start()
    cot_h.shift_local()
    lay_adjoint(two_ref, two_adj)
    convolve_local(cot_f, two_adj, 0, grad_act)
    clip_h.receive()
    clip_h.shift_rim()

    def emit_hidden(fr, rr, value):
        hidden = value + bias_ref[...]
        sig = 1.0 / (1.0 + jnp.exp(-hidden))
        act_f[fr + 2, rr + 1, mid] = (hidden * sig).astype(jnp.bfloat16)
        slope[fr, rr] = sig * (1.0 + hidden * (1.0 - sig))

    convolve_rest(clip_f, one_w, 2, slope, emit_hidden)
    act_h.start()
    act_h.shift_local()

    cot_h.receive()
    cot_h.shift_rim()
    bias_sum[...] = jnp.zeros(bias_sum.shape, jnp.float32)

    def emit_pre(fr, rr, value):
        pre = (value * slope[fr, rr]).astype(jnp.bfloat16)
        pre_f[fr, rr + 1, mid] = pre
        bias_sum[...] += pre.astype(jnp.float32)

    convolve_rest(cot_f, two_adj, 0, grad_act, emit_pre)
    pre_h.start()

    wide = one_w.shape[1] // LANES
    tall = one_w.shape[0]
    used = wide * tall + chan
    reductions = [
        Reduction(
            [buf.at[k] for buf in (send, got_f, part, total, got_r, full)],
            reduce_sems.at[k], sizes, place,
        )
        for k in range(2)
    ]
    bias_term = jnp.sum(bias_sum[...], axis=1, keepdims=True)
    bias_rows = jnp.broadcast_to(bias_term, (chan, LANES)).astype(jnp.bfloat16)
    rest = send.shape[1] - used

    def reduce_grad(k):
        flipped = jnp.transpose(grad_sum[...])
        for b in range(wide):
            send[k, pl.ds(b * tall, tall)] = flipped[:tall, b * LANES : (b + 1) * LANES].astype(
                jnp.bfloat16
            )
        send[k, pl.ds(used - chan, chan)] = bias_rows
        if rest:
            send[k, pl.ds(used, rest)] = jnp.zeros((rest, LANES), jnp.bfloat16)
        reductions[k].scatter_frames()

    kernel_grad(pre_f, clip_f, grad_sum)
    reduce_grad(0)
    act_h.receive()
    act_h.shift_rim()
    kernel_grad(cot_f, act_f, grad_sum)
    reduce_grad(1)
    reductions[0].scatter_rows()
    lay_forward(two_ref, two_w)
    lay_adjoint(one_ref, one_adj)
    pre_h.shift_local()

    def emit_block(fr, rr, value):
        block_ref[fr, rr] = (clip_f[fr + 2, rr + 1, mid].astype(jnp.float32) + value).astype(jnp.bfloat16)

    half_way = row_count // 2
    convolve(act_f, two_w, emit_block, (0, half_way, 1))
    reductions[0].gather_rows()
    convolve(act_f, two_w, emit_block, (half_way, 1, 1))
    reductions[1].scatter_rows()
    convolve(act_f, two_w, emit_block, (half_way + 1, row_count - half_way - 1, 1))
    stores[0].start()
    reductions[0].gather_frames()

    pre_h.receive()
    pre_h.shift_rim()

    def emit_input(fr, rr, value):
        input_ref[fr, rr] = (cot_f[fr, rr + 1, mid].astype(jnp.float32) + value).astype(jnp.bfloat16)

    convolve(pre_f, one_adj, emit_input, (0, half_way, 1))
    reductions[1].gather_rows()
    convolve(pre_f, one_adj, emit_input, (half_way, 1, 1))
    reductions[1].gather_frames()
    convolve(pre_f, one_adj, emit_input, (half_way + 1, row_count - half_way - 1, 1))

    stores[1].start()
    for k, out in enumerate((first_ref, second_ref)):
        reductions[k].finish()
        for t in range(3):
            for tap in range(9):
                lane = tap * chan
                b, inner = lane // LANES, lane % LANES
                tile = full[k, pl.ds(b * tall + t * chan, chan)]
                out[t, tap // 3, tap % 3] = (
                    tile[:, inner : inner + chan].astype(jnp.float32) * inv_scale
                )
        stores[2 + k].start()
    bias_out_ref[...] = full[0, pl.ds(used - chan, chan)].astype(jnp.float32) * inv_scale
    for reduction in reductions:
        reduction.drain()
    for halo in (clip_h, cot_h, act_h, pre_h):
        halo.drain()
    for store in stores:
        store.wait()


def per_device(clip_in, kernel_one, bias_one, kernel_two, cotangent):
    frame_count, row_count, chan, cols = clip_in.shape
    frames, rows = lax.axis_size("frames"), lax.axis_size("rows")
    inv_scale = 1.0 / math.sqrt(frame_count * frames * row_count * rows * cols)

    wide = -(-9 * chan // LANES)
    tall = 3 * chan
    count = wide * tall + chan
    count += -count % (frames * rows * 16)
    chunk_f = count // frames
    chunk_r = chunk_f // rows
    dma = pltpu.SemaphoreType.DMA
    bf16, f32 = jnp.bfloat16, jnp.float32
    field = pltpu.VMEM((frame_count + 2, row_count + 2, 3 * chan, cols), bf16)
    weights = pltpu.VMEM((tall, wide * LANES), bf16)
    vmem = pl.BlockSpec(memory_space=pltpu.VMEM)
    hbm = pl.BlockSpec(memory_space=pltpu.HBM)
    block, grad_input, first, second, bias = pl.pallas_call(
        functools.partial(block_kernel, frames, rows, inv_scale),
        out_shape=(
            jax.ShapeDtypeStruct(clip_in.shape, bf16),
            jax.ShapeDtypeStruct(clip_in.shape, bf16),
            jax.ShapeDtypeStruct(kernel_one.shape, f32),
            jax.ShapeDtypeStruct(kernel_two.shape, f32),
            jax.ShapeDtypeStruct((chan, LANES), f32),
        ),
        in_specs=[hbm] * 5,
        out_specs=(hbm,) * 4 + (vmem,),
        scratch_shapes=[
            pltpu.VMEM(clip_in.shape, bf16),
            pltpu.VMEM(clip_in.shape, bf16),
            pltpu.VMEM(kernel_one.shape, f32),
            pltpu.VMEM(kernel_two.shape, f32),
            dma((4,)),
            pltpu.VMEM(kernel_one.shape, bf16),
            pltpu.VMEM(kernel_two.shape, bf16),
            pltpu.VMEM((chan, 1), f32),
            dma((5,)),
            field, field, field, field,
            pltpu.VMEM(clip_in.shape, f32),
            pltpu.VMEM(clip_in.shape, f32),
            weights, weights, weights, weights,
            pltpu.VMEM((wide * LANES, -(-tall // LANES) * LANES), f32),
            pltpu.VMEM((chan, cols), f32),
            pltpu.VMEM((2, count, LANES), bf16),
            pltpu.VMEM((2, frames - 1, chunk_f, LANES), bf16),
            pltpu.VMEM((2, chunk_f, LANES), bf16),
            pltpu.VMEM((2, chunk_f, LANES), f32),
            pltpu.VMEM((2, rows - 1, chunk_r, LANES), bf16),
            pltpu.VMEM((2, count, LANES), bf16),
            dma((4, 2, 5)),
            dma((2, 4, 2, max(frames, rows) - 1)),
        ],
        compiler_params=pltpu.CompilerParams(
            collective_id=0, has_side_effects=True, vmem_limit_bytes=62 * 1024 * 1024
        ),
    )(
        clip_in, cotangent, kernel_one, kernel_two, bias_one.reshape((chan, 1)),
    )
    return block, grad_input, first, second, bias[:, 0]


def solution(mesh):
    in_specs = (P("frames", "rows", None, None), P(), P(), P(), P("frames", "rows", None, None))
    out_specs = (P("frames", "rows", None, None), P("frames", "rows", None, None), P(), P(), P())
    return jax.shard_map(
        per_device, mesh=mesh, in_specs=in_specs, out_specs=out_specs, check_vma=False
    )
```

```python
import functools
import math

import jax
import jax.numpy as jnp
from jax import lax
from jax.experimental import pallas as pl
from jax.experimental.pallas import tpu as pltpu
from jax.sharding import PartitionSpec as P

MESH = pl.DeviceIdType.MESH
LANES = 128


def remote(src, dst, send_sem, recv_sem, device):
    return pltpu.make_async_remote_copy(
        src_ref=src,
        dst_ref=dst,
        send_sem=send_sem,
        recv_sem=recv_sem,
        device_id=device,
        device_id_type=MESH,
    )


class Halo:
    def __init__(self, field, sems, later, sizes, place):
        self.field, self.later = field, later
        frames, rows = sizes
        f, r = place
        self.frame_count, self.row_count = field.shape[0] - 2, field.shape[1] - 2
        chan = self.chan = field.shape[2] // 3
        fc, rc = self.frame_count, self.row_count
        mid = pl.ds(chan, chan)
        self.first = 0 if later else 2
        local = pl.ds(self.first, fc)
        edge, rim = (pl.ds(0, 2), pl.ds(fc, 2)) if later else (pl.ds(fc, 2), pl.ds(0, 2))
        self.rim_first = fc if later else 0
        up, down = lax.rem(r + 1, rows), lax.rem(r + rows - 1, rows)
        side = lax.rem(f + (frames - 1 if later else 1), frames)
        to_up, to_down = r < rows - 1, r > 0
        to_side, from_side = (f > 0, f < frames - 1) if later else (f < frames - 1, f > 0)
        self.items = []
        plan = [
            (local, rc, local, 0, (f, up), to_up, to_down),
            (local, 1, local, rc + 1, (f, down), to_down, to_up),
            (edge, pl.ds(1, rc), rim, pl.ds(1, rc), (side, r), to_side, from_side),
            (edge, rc, rim, 0, (side, up), to_side & to_up, from_side & to_down),
            (edge, 1, rim, rc + 1, (side, down), to_side & to_down, from_side & to_up),
        ]
        for n, (se, sr, de, dr, device, sends, gets) in enumerate(plan):
            target = field.at[de, dr, mid]
            copy = remote(field.at[se, sr, mid], target, sems.at[0, n], sems.at[1, n], device)
            self.items.append((copy, target, sends, gets))

    def start(self):
        for copy, _, sends, _ in self.items:
            pl.when(sends)(copy.start)

    def shift(self, first, count, rows):
        field, chan = self.field, self.chan

        def body(e, carry):
            for row in rows:
                value = field[e, row, chan : 2 * chan]
                cols = value.shape[1]
                blank = jnp.zeros((chan, 1), value.dtype)
                field[e, row, 0:chan] = jnp.concatenate([blank, value[:, : cols - 1]], axis=1)
                field[e, row, 2 * chan : 3 * chan] = jnp.concatenate([value[:, 1:], blank], axis=1)
            return carry

        lax.fori_loop(first, first + count, body, 0)

    def shift_local(self):
        self.shift(self.first, self.frame_count, range(1, self.row_count + 1))

    def receive(self):
        for copy, target, _, gets in self.items:
            pl.when(gets)(copy.wait_recv)

            def clear(target=target):
                target[...] = jnp.zeros(target.shape, jnp.bfloat16)

            pl.when(jnp.logical_not(gets))(clear)

    def shift_rim(self):
        self.shift(self.first, self.frame_count, (0, self.row_count + 1))
        self.shift(self.rim_first, 2, range(self.row_count + 2))

    def drain(self):
        for copy, _, sends, _ in self.items:
            pl.when(sends)(copy.wait_send)


def offsets(e, frame_count):
    return max(0, e - frame_count + 1), min(2, e)


def convolve(field, weights, emit, rows, frames=None, base=None):
    frame_count = field.shape[0] - 2
    chan, cols = field.shape[2] // 3, field.shape[3]
    start, count, step = rows

    def body(k, carry):
        r = start + k * step
        sums = [None if base is None else base[f, r] for f in range(frame_count)]
        for e in range(frame_count + 2) if frames is None else frames:
            low, high = offsets(e, frame_count)
            taps = field[e, pl.ds(r, 3)].reshape((9 * chan, cols))
            part = jnp.dot(
                weights[low * chan : (high + 1) * chan, 0 : 9 * chan],
                taps,
                preferred_element_type=jnp.float32,
            )
            for t in range(low, high + 1):
                term = part[(t - low) * chan : (t - low + 1) * chan]
                sums[e - t] = term if sums[e - t] is None else sums[e - t] + term
        for f in range(frame_count):
            emit(f, r, sums[f])
        return carry

    lax.fori_loop(0, count, body, 0)


def convolve_local(field, weights, first, partial):
    frame_count, row_count = field.shape[0] - 2, field.shape[1] - 2

    def keep(f, r, value):
        partial[f, r] = value

    convolve(
        field, weights, keep, (1, row_count - 2, 1), range(first, first + frame_count)
    )


def convolve_rest(field, weights, first, partial, emit):
    frame_count, row_count = field.shape[0] - 2, field.shape[1] - 2
    rim = [e for e in range(frame_count + 2) if not first <= e < first + frame_count]
    convolve(field, weights, emit, (1, row_count - 2, 1), rim, partial)
    convolve(field, weights, emit, (0, 2, row_count - 1))


def kernel_grad(upstream, field, total):
    frame_count, row_count = field.shape[0] - 2, field.shape[1] - 2
    chan, cols = field.shape[2] // 3, field.shape[3]
    total[...] = jnp.zeros(total.shape, jnp.float32)
    blank = jnp.zeros((chan, row_count * cols), jnp.bfloat16)
    for e in range(frame_count + 2):
        low, high = offsets(e, frame_count)
        taps = jnp.concatenate(
            [field[e, r : r + 3].reshape((9 * chan, cols)) for r in range(row_count)], axis=1
        )
        right = []
        for t in range(3):
            if low <= t <= high:
                lines = [upstream[e - t, r + 1, chan : 2 * chan] for r in range(row_count)]
                right.append(jnp.concatenate(lines, axis=1))
            else:
                right.append(blank)
        total[0 : 9 * chan, 0 : 3 * chan] += lax.dot_general(
            taps,
            jnp.concatenate(right, axis=0),
            (((1,), (1,)), ((), ())),
            preferred_element_type=jnp.float32,
        )


def lay_forward(kernel, weights):
    chan = kernel.shape[3]
    for t in range(3):
        for tap in range(9):
            weights[t * chan : (t + 1) * chan, tap * chan : (tap + 1) * chan] = kernel[
                t, tap // 3, tap % 3
            ]


def lay_adjoint(kernel, weights):
    chan = kernel.shape[3]
    for t in range(3):
        for tap in range(9):
            piece = kernel[2 - t, 2 - tap // 3, 2 - tap % 3].astype(jnp.float32)
            weights[t * chan : (t + 1) * chan, tap * chan : (tap + 1) * chan] = jnp.transpose(
                piece
            ).astype(jnp.bfloat16)


class Reduction:
    def __init__(self, bufs, sems, sizes, place):
        self.send, self.got_f, self.part, self.total, self.got_r, self.full = bufs
        self.sems = sems
        self.sizes, self.place = sizes, place
        frames, rows = sizes
        f, r = place
        self.chunk_f = self.send.shape[0] // frames
        self.chunk_r = self.chunk_f // rows
        self.own_f = pl.multiple_of(f * self.chunk_f, self.chunk_f)
        self.frame_peers = [lax.rem(f + d, frames) for d in range(1, frames)]
        self.row_peers = [lax.rem(r + d, rows) for d in range(1, rows)]

    def copy(self, src, dst, kind, n, device):
        return remote(src, dst, self.sems.at[kind, 0, n], self.sems.at[kind, 1, n], device)

    def scatter_frames(self):
        _, r = self.place
        self.first = []
        for n, p in enumerate(self.frame_peers):
            at = pl.ds(pl.multiple_of(p * self.chunk_f, self.chunk_f), self.chunk_f)
            self.first.append(self.copy(self.send.at[at], self.got_f.at[n], 0, n, (p, r)))
            self.first[-1].start()

    def scatter_rows(self):
        f, _ = self.place
        value = self.send[pl.ds(self.own_f, self.chunk_f)].astype(jnp.float32)
        for n, copy in enumerate(self.first):
            copy.wait_recv()
            value = value + self.got_f[n].astype(jnp.float32)
        self.total[...] = value
        self.part[...] = value.astype(jnp.bfloat16)
        self.second = []
        for n, q in enumerate(self.row_peers):
            at = pl.ds(pl.multiple_of(q * self.chunk_r, self.chunk_r), self.chunk_r)
            self.second.append(self.copy(self.part.at[at], self.got_r.at[n], 1, n, (f, q)))
            self.second[-1].start()

    def gather_rows(self):
        f, r = self.place
        own = pl.multiple_of(r * self.chunk_r, self.chunk_r)
        value = self.total[pl.ds(own, self.chunk_r)]
        for n, copy in enumerate(self.second):
            copy.wait_recv()
            value = value + self.got_r[n].astype(jnp.float32)
        at = pl.multiple_of(f * self.chunk_f + r * self.chunk_r, self.chunk_r)
        here = self.full.at[pl.ds(at, self.chunk_r)]
        here[...] = value.astype(jnp.bfloat16)
        self.third = []
        for n, q in enumerate(self.row_peers):
            self.third.append(self.copy(here, here, 2, n, (f, q)))
            self.third[-1].start()

    def gather_frames(self):
        _, r = self.place
        for copy in self.third:
            copy.wait_recv()
        block = self.full.at[pl.ds(self.own_f, self.chunk_f)]
        self.fourth = []
        for n, p in enumerate(self.frame_peers):
            self.fourth.append(self.copy(block, block, 3, n, (p, r)))
            self.fourth[-1].start()

    def finish(self):
        for copy in self.fourth:
            copy.wait_recv()

    def drain(self):
        for copy in self.first + self.second + self.third + self.fourth:
            copy.wait_send()


def block_kernel(
    frames, rows, inv_scale,
    clip_hbm, cot_hbm, one_hbm, two_hbm, bias_hbm,
    block_hbm, input_hbm, first_hbm, second_hbm, bias_out_ref,
    block_ref, input_ref, first_ref, second_ref, out_sems,
    one_ref, two_ref, bias_row, bias_ref, local_sems,
    clip_f, cot_f, act_f, pre_f, slope, grad_act, one_w, two_w, one_adj, two_adj, grad_sum, bias_sum,
    send, got_f, part, total, got_r, full,
    halo_sems, reduce_sems,
):
    f, r = lax.axis_index("frames"), lax.axis_index("rows")
    frame_count, row_count, chan, cols = clip_hbm.shape
    place, sizes = (f, r), (frames, rows)

    mid = slice(chan, 2 * chan)
    inner = pl.ds(1, row_count), pl.ds(chan, chan)
    loads = [
        pltpu.make_async_copy(src, dst, local_sems.at[n])
        for n, (src, dst) in enumerate(
            (
                (clip_hbm, clip_f.at[pl.ds(2, frame_count), *inner]),
                (one_hbm, one_ref),
                (bias_hbm, bias_row),
                (cot_hbm, cot_f.at[pl.ds(0, frame_count), *inner]),
                (two_hbm, two_ref),
            )
        )
    ]
    for load in loads:
        load.start()
    stores = [
        pltpu.make_async_copy(src, dst, out_sems.at[n])
        for n, (src, dst) in enumerate(
            (
                (block_ref, block_hbm),
                (input_ref, input_hbm),
                (first_ref, first_hbm),
                (second_ref, second_hbm),
            )
        )
    ]
    barrier = pltpu.get_barrier_semaphore()
    others = [(lax.rem(f + d, frames), r) for d in range(1, frames)]
    others += [(f, lax.rem(r + d, rows)) for d in range(1, rows)]
    for df in (1, frames - 1):
        for dr in (1, rows - 1):
            others.append((lax.rem(f + df, frames), lax.rem(r + dr, rows)))
    for device in others:
        pl.semaphore_signal(barrier, inc=1, device_id=device, device_id_type=MESH)
    loads[0].wait()
    pl.semaphore_wait(barrier, len(others))

    clip_h = Halo(clip_f, halo_sems.at[0], False, sizes, place)
    cot_h = Halo(cot_f, halo_sems.at[1], True, sizes, place)
    act_h = Halo(act_f, halo_sems.at[2], False, sizes, place)
    pre_h = Halo(pre_f, halo_sems.at[3], True, sizes, place)
    clip_h.start()
    loads[1].wait()
    lay_forward(one_ref, one_w)
    clip_h.shift_local()
    convolve_local(clip_f, one_w, 2, slope)
    for load in loads[2:]:
        load.wait()
    cot_h.start()
    cot_h.shift_local()
    lay_adjoint(two_ref, two_adj)
    column = jnp.transpose(jnp.broadcast_to(bias_row[...], (LANES, chan)))[:, 0:1]
    bias_ref[...] = jnp.broadcast_to(column, bias_ref.shape)
    convolve_local(cot_f, two_adj, 0, grad_act)
    clip_h.receive()
    clip_h.shift_rim()

    def emit_hidden(fr, rr, value):
        hidden = value + bias_ref[...]
        sig = 1.0 / (1.0 + jnp.exp(-hidden))
        act_f[fr + 2, rr + 1, mid] = (hidden * sig).astype(jnp.bfloat16)
        slope[fr, rr] = sig * (1.0 + hidden * (1.0 - sig))

    convolve_rest(clip_f, one_w, 2, slope, emit_hidden)
    act_h.start()
    act_h.shift_local()

    cot_h.receive()
    cot_h.shift_rim()
    bias_sum[...] = jnp.zeros(bias_sum.shape, jnp.float32)

    def emit_pre(fr, rr, value):
        pre = (value * slope[fr, rr]).astype(jnp.bfloat16)
        pre_f[fr, rr + 1, mid] = pre
        bias_sum[...] += pre.astype(jnp.float32)

    convolve_rest(cot_f, two_adj, 0, grad_act, emit_pre)
    pre_h.start()

    wide = one_w.shape[1] // LANES
    tall = one_w.shape[0]
    used = wide * tall + chan
    reductions = [
        Reduction(
            [buf.at[k] for buf in (send, got_f, part, total, got_r, full)],
            reduce_sems.at[k], sizes, place,
        )
        for k in range(2)
    ]
    bias_term = jnp.sum(bias_sum[...], axis=1, keepdims=True)
    bias_rows = jnp.broadcast_to(bias_term, (chan, LANES)).astype(jnp.bfloat16)
    rest = send.shape[1] - used

    def reduce_grad(k):
        flipped = jnp.transpose(grad_sum[...])
        for b in range(wide):
            send[k, pl.ds(b * tall, tall)] = flipped[:tall, b * LANES : (b + 1) * LANES].astype(
                jnp.bfloat16
            )
        send[k, pl.ds(used - chan, chan)] = bias_rows
        if rest:
            send[k, pl.ds(used, rest)] = jnp.zeros((rest, LANES), jnp.bfloat16)
        reductions[k].scatter_frames()

    kernel_grad(pre_f, clip_f, grad_sum)
    reduce_grad(0)
    act_h.receive()
    act_h.shift_rim()
    kernel_grad(cot_f, act_f, grad_sum)
    reduce_grad(1)
    reductions[0].scatter_rows()
    lay_forward(two_ref, two_w)
    lay_adjoint(one_ref, one_adj)
    pre_h.shift_local()

    def emit_block(fr, rr, value):
        block_ref[fr, rr] = (clip_f[fr + 2, rr + 1, mid].astype(jnp.float32) + value).astype(jnp.bfloat16)

    half_way = row_count // 2
    convolve(act_f, two_w, emit_block, (0, half_way, 1))
    reductions[0].gather_rows()
    convolve(act_f, two_w, emit_block, (half_way, 1, 1))
    reductions[1].scatter_rows()
    convolve(act_f, two_w, emit_block, (half_way + 1, row_count - half_way - 1, 1))
    stores[0].start()
    reductions[0].gather_frames()

    pre_h.receive()
    pre_h.shift_rim()

    def emit_input(fr, rr, value):
        input_ref[fr, rr] = (cot_f[fr, rr + 1, mid].astype(jnp.float32) + value).astype(jnp.bfloat16)

    convolve(pre_f, one_adj, emit_input, (0, half_way, 1))
    reductions[1].gather_rows()
    convolve(pre_f, one_adj, emit_input, (half_way, 1, 1))
    reductions[1].gather_frames()
    convolve(pre_f, one_adj, emit_input, (half_way + 1, row_count - half_way - 1, 1))

    stores[1].start()
    for k, out in enumerate((first_ref, second_ref)):
        reductions[k].finish()
        for t in range(3):
            for tap in range(9):
                lane = tap * chan
                b, inner = lane // LANES, lane % LANES
                tile = full[k, pl.ds(b * tall + t * chan, chan)]
                out[t, tap // 3, tap % 3] = (
                    tile[:, inner : inner + chan].astype(jnp.float32) * inv_scale
                )
        stores[2 + k].start()
    bias_tile = full[0, pl.ds(used - chan, chan)].astype(jnp.float32) * inv_scale
    bias_out_ref[...] = jnp.transpose(bias_tile)[0:1]
    for reduction in reductions:
        reduction.drain()
    for halo in (clip_h, cot_h, act_h, pre_h):
        halo.drain()
    for store in stores:
        store.wait()


def per_device(clip_in, kernel_one, bias_one, kernel_two, cotangent):
    frame_count, row_count, chan, cols = clip_in.shape
    frames, rows = lax.axis_size("frames"), lax.axis_size("rows")
    inv_scale = 1.0 / math.sqrt(frame_count * frames * row_count * rows * cols)

    wide = -(-9 * chan // LANES)
    tall = 3 * chan
    count = wide * tall + chan
    count += -count % (frames * rows * 16)
    chunk_f = count // frames
    chunk_r = chunk_f // rows
    dma = pltpu.SemaphoreType.DMA
    bf16, f32 = jnp.bfloat16, jnp.float32
    field = pltpu.VMEM((frame_count + 2, row_count + 2, 3 * chan, cols), bf16)
    weights = pltpu.VMEM((tall, wide * LANES), bf16)
    vmem = pl.BlockSpec(memory_space=pltpu.VMEM)
    hbm = pl.BlockSpec(memory_space=pltpu.HBM)
    block, grad_input, first, second, bias = pl.pallas_call(
        functools.partial(block_kernel, frames, rows, inv_scale),
        out_shape=(
            jax.ShapeDtypeStruct(clip_in.shape, bf16),
            jax.ShapeDtypeStruct(clip_in.shape, bf16),
            jax.ShapeDtypeStruct(kernel_one.shape, f32),
            jax.ShapeDtypeStruct(kernel_two.shape, f32),
            jax.ShapeDtypeStruct((1, chan), f32),
        ),
        in_specs=[hbm] * 5,
        out_specs=(hbm,) * 4 + (vmem,),
        scratch_shapes=[
            pltpu.VMEM(clip_in.shape, bf16),
            pltpu.VMEM(clip_in.shape, bf16),
            pltpu.VMEM(kernel_one.shape, f32),
            pltpu.VMEM(kernel_two.shape, f32),
            dma((4,)),
            pltpu.VMEM(kernel_one.shape, bf16),
            pltpu.VMEM(kernel_two.shape, bf16),
            pltpu.VMEM((1, chan), f32),
            pltpu.VMEM((chan, cols), f32),
            dma((5,)),
            field, field, field, field,
            pltpu.VMEM(clip_in.shape, f32),
            pltpu.VMEM(clip_in.shape, f32),
            weights, weights, weights, weights,
            pltpu.VMEM((wide * LANES, -(-tall // LANES) * LANES), f32),
            pltpu.VMEM((chan, cols), f32),
            pltpu.VMEM((2, count, LANES), bf16),
            pltpu.VMEM((2, frames - 1, chunk_f, LANES), bf16),
            pltpu.VMEM((2, chunk_f, LANES), bf16),
            pltpu.VMEM((2, chunk_f, LANES), f32),
            pltpu.VMEM((2, rows - 1, chunk_r, LANES), bf16),
            pltpu.VMEM((2, count, LANES), bf16),
            dma((4, 2, 5)),
            dma((2, 4, 2, max(frames, rows) - 1)),
        ],
        compiler_params=pltpu.CompilerParams(
            collective_id=0, has_side_effects=True, vmem_limit_bytes=62 * 1024 * 1024
        ),
    )(
        clip_in, cotangent, kernel_one, kernel_two, bias_one.reshape((1, chan)),
    )
    return block, grad_input, first, second, bias.reshape((chan,))


def solution(mesh):
    in_specs = (P("frames", "rows", None, None), P(), P(), P(), P("frames", "rows", None, None))
    out_specs = (P("frames", "rows", None, None), P("frames", "rows", None, None), P(), P(), P())
    return jax.shard_map(
        per_device, mesh=mesh, in_specs=in_specs, out_specs=out_specs, check_vma=False
    )
```
